768 devices in a mesh: blk: 192 (over y_lo, z, x), grp: 4 (over y_hi, core).
Axes of the slice: x: 4, y: 8 (y_hi: 2, y_lo: 4; y = y_hi * 4 + y_lo), z: 12, core: 2. Of those that a mesh axis runs over, the one named last changes fastest.
Arguments:
- images: bfloat16 [196608, 1152], P(('blk', 'grp')), may hold values from -6 to 6
- texts: bfloat16 [196608, 1152], P(('blk', 'grp')), may hold values from -6 to 6
- row_weight: float32 [196608], P('blk'), may hold values from 0.05 to 0.5
- log_sharpness_parameter: float32 [1], replicated, may hold values from 2.3 to 2.9
- bias: float32 [1], replicated, may hold values from -2 to -0.5
Outputs:
- image_grad: float32 [196608, 1152], P(('blk', 'grp'))
- text_grad: bfloat16 [196608, 1152], P(('blk', 'grp'))
- row_loss: float32 [196608], P(('blk', 'grp'))
The draws below stay inside these ranges and needn't reach their ends.
All inputs are finite; a program needn't handle non-finite values.
Results may differ from the reference program's by a relative error of at most 0.015.
Values may be sent and summed in bfloat16 or wider, within the bound.
A program may use at most 64 MiB of HBM per device.

```python
import math
import jax
import jax.numpy as jnp
from jax import lax

D = 1152
IMG_DEV = 256
STEPS = 2
PAIRS = 196608
N_BLK = 192
N_GRP = 4


def block_levels(own_key, extent, pieces, smallest, largest):
    loudness, own = 1.0, jax.random.fold_in(own_key, 6)
    for axis_at, shards_of in pieces:
        draws = jnp.exp(jax.random.uniform(jax.random.fold_in(own, axis_at), (shards_of,), jnp.float32, smallest / len(pieces), largest / len(pieces)))
        loudness = loudness * jnp.repeat(draws, extent[axis_at] // shards_of).reshape([-1 if axis == axis_at else 1 for axis in range(len(extent))])
    return loudness


def normal_values(key, extent, spread, most, shards=(), kind=jnp.bfloat16):
    loudness = block_levels(key, extent, shards, -0.22, 0.18) if shards else 1.0
    result = jax.random.normal(key, extent, jnp.float32) * spread * loudness
    return jnp.minimum(jnp.maximum(result, -most), most).astype(kind)


def setup_inputs(seed: int = 0) -> dict:
    key_of = jax.random.split(jax.random.key(seed), 6)
    return {
        "images": normal_values(key_of[0], (PAIRS, D), 1.0, 6.0, ((0, 768),)),
        "texts": normal_values(key_of[1], (PAIRS, D), 1.0, 6.0, ((0, 768),)),
        "row_weight": jnp.clip(jnp.exp(math.log(0.5) - 2.3025851 * jax.random.uniform(key_of[2], (PAIRS,), jnp.float32) ** block_levels(key_of[2], (PAIRS,), ((0, 192),), -0.2, 0.2)), 0.05, 0.5),
        "log_sharpness_parameter": jnp.clip(jax.random.uniform(key_of[3], (1,), jnp.float32, 2.3, 2.9), 2.3, 2.9),
        "bias": jnp.clip(jax.random.uniform(key_of[4], (1,), jnp.float32, -2.0, -0.5), -2.0, -0.5),
    }


def normalize(raw):
    values = raw.astype(jnp.float32)
    inverse = lax.rsqrt(lax.optimization_barrier(jnp.sum(values * values, axis=-1, keepdims=True)) + 1e-06)
    return (values * inverse, inverse)

def reference(images, texts, row_weight, log_sharpness_parameter, bias):
    group_rows = IMG_DEV * N_GRP
    sharpness_factor = jnp.exp(log_sharpness_parameter[0])
    segment_start_index = bias[0]
    normed, inverse = normalize(images)
    normed_b = normed.astype(jnp.bfloat16)
    text_unit = normalize(texts)[0].astype(jnp.bfloat16)
    local_index = jnp.arange(group_rows, dtype=jnp.int32)

    def visit_block(carry, owner_block):
        picture_gradient_step, loss_sum = carry
        source = (owner_block - (STEPS - 1)) % N_BLK
        text_first_row = (source * group_rows).astype(jnp.int32)
        caption_segment_entries = lax.dynamic_slice_in_dim(text_unit, text_first_row, group_rows, 0)
        text_index = text_first_row + local_index
        carried = jnp.zeros((group_rows, D), jnp.bfloat16)
        for visit in range(STEPS):
            image_group = (source + visit) % N_BLK
            image_first_row = (image_group * group_rows).astype(jnp.int32)
            picture_segment_entries = lax.dynamic_slice_in_dim(normed_b, image_first_row, group_rows, 0)
            model_weights = lax.dynamic_slice_in_dim(row_weight, image_first_row, group_rows, 0)
            affinity_scores_matrix = sharpness_factor * jnp.dot(picture_segment_entries, caption_segment_entries.T, preferred_element_type=jnp.float32) + segment_start_index
            positive = ((image_first_row + local_index)[:, None] == text_index[None, :]).astype(jnp.float32)
            losses = lax.optimization_barrier(jnp.sum(jax.nn.softplus((1.0 - 2.0 * positive) * affinity_scores_matrix), axis=1))
            grad_logit = (model_weights[:, None] * (jax.nn.sigmoid(affinity_scores_matrix) - positive)).astype(jnp.bfloat16)
            negative_gradient_direction = jnp.dot(grad_logit, caption_segment_entries, preferred_element_type=jnp.float32)
            divided_pieces_count = jnp.einsum('kic,kid->kcd', grad_logit.reshape(N_GRP, IMG_DEV, group_rows).astype(jnp.float32), picture_segment_entries.reshape(N_GRP, IMG_DEV, D).astype(jnp.float32))
            narrowed_precision_output = lax.optimization_barrier((sharpness_factor * divided_pieces_count).astype(jnp.bfloat16))
            carried = (carried.astype(jnp.float32) + lax.optimization_barrier(jnp.sum(narrowed_precision_output.astype(jnp.float32), axis=0))).astype(jnp.bfloat16)
            old_dir = lax.dynamic_slice_in_dim(picture_gradient_step, image_first_row, group_rows, 0)
            picture_gradient_step = lax.dynamic_update_slice_in_dim(picture_gradient_step, old_dir + negative_gradient_direction, image_first_row, 0)
            old_loss = lax.dynamic_slice_in_dim(loss_sum, image_first_row, group_rows, 0)
            loss_sum = lax.dynamic_update_slice_in_dim(loss_sum, old_loss + losses, image_first_row, 0)
        return ((picture_gradient_step, loss_sum), carried)
    start_state = (jnp.zeros((PAIRS, D), jnp.float32), jnp.zeros((PAIRS,), jnp.float32))
    (picture_gradient_step, loss_sum), blocks = lax.scan(visit_block, start_state, jnp.arange(N_BLK, dtype=jnp.int32))
    text_grad = blocks.reshape(PAIRS, D)
    multiplied_gradient_step = sharpness_factor * picture_gradient_step
    image_grad = inverse * (multiplied_gradient_step - normed * lax.optimization_barrier(jnp.sum(normed * multiplied_gradient_step, axis=-1, keepdims=True)))
    row_loss = loss_sum / (STEPS * group_rows)
    return (image_grad, text_grad, row_loss)
```

```python
import functools

import jax
import jax.numpy as jnp
from jax import lax
from jax.experimental import pallas as pl
from jax.experimental.pallas import tpu as pltpu
from jax.sharding import PartitionSpec as P

MESH = pl.DeviceIdType.MESH
STEPS = 2
ROWS = 256
CHUNK = 64
CHUNKS = ROWS // CHUNK
WIDE = 128
PLANE = 48
RELAYS = 16
RELAY_PLACE = 28
PIECE = ROWS // RELAYS
HELD = 2
EPS = 1e-06


def kernel(
    features,
    sharp_ref,
    bias_ref,
    weights_hbm,
    images_hbm,
    texts_hbm,
    image_grad_ref,
    text_grad_ref,
    row_loss_ref,
    images_ref,
    texts_ref,
    weight_ref,
    near,
    far,
    text,
    grads_near,
    grads_far,
    inverse,
    own_dir,
    near_out,
    near_in,
    far_out,
    far_in,
    back_out,
    back_in,
    carry_out,
    carry_in,
    relay,
    loss_out,
    loss_in,
    far_loss,
    text_sum,
    s_near,
    s_far,
    s_text,
    s_fwd,
    s_ndir,
    s_fdir,
    s_back,
    s_carry,
    s_loss,
    s_relay,
    s_load,
):
    loads = [
        pltpu.make_async_copy(
            images_hbm.at[pl.ds(0, CHUNK)], images_ref.at[pl.ds(0, CHUNK)], s_load.at[0]
        ),
        pltpu.make_async_copy(texts_hbm, texts_ref, s_load.at[1]),
        pltpu.make_async_copy(
            images_hbm.at[pl.ds(CHUNK, ROWS - CHUNK)],
            images_ref.at[pl.ds(CHUNK, ROWS - CHUNK)],
            s_load.at[2],
        ),
        pltpu.make_async_copy(weights_hbm, weight_ref, s_load.at[3]),
    ]
    for one in loads:
        one.start()
    blk = lax.axis_index("blk")
    member = lax.axis_index("grp")
    groups = lax.axis_size("blk")
    sibling = member + 1 - 2 * lax.rem(member, 2)
    opposite = lax.rem(member + 2, 4)
    diagonal = lax.rem(sibling + 2, 4)
    at_grp = lambda g: {"blk": blk, "grp": g}
    at_blk = lambda b: {"blk": b, "grp": member}
    ahead = lax.rem(blk + 1, groups)
    behind = lax.rem(blk + groups - 1, groups)
    place = lax.rem(blk, PLANE)
    base = blk - place
    next_base = lax.rem(base + PLANE, groups)
    last_base = lax.rem(base + groups - PLANE, groups)
    is_last = place == PLANE - 1
    is_first = place == 0
    piece = place - RELAY_PLACE
    is_relay = (piece >= 0) & (piece < RELAYS)
    relay_place = lambda j: RELAY_PLACE + j

    def copy(src, dst, sems, k, device):
        return pltpu.make_async_remote_copy(
            src_ref=src,
            dst_ref=dst,
            send_sem=sems.at[0, k],
            recv_sem=sems.at[1, k],
            device_id=device,
            device_id_type=MESH,
        )

    barrier = pltpu.get_barrier_semaphore()

    def greet(device):
        pl.semaphore_signal(barrier, inc=1, device_id=device, device_id_type=MESH)

    for other in (sibling, opposite, diagonal):
        greet(at_grp(other))

    @pl.when(is_first)
    def _():
        for j in range(RELAYS):
            greet(at_blk(base + relay_place(j)))

    @pl.when(jnp.logical_not(is_first))
    def _():
        greet(at_blk(behind))

    @pl.when(is_relay)
    def _():
        greet(at_blk(base + PLANE - 1))
        greet(at_blk(last_base + place))

    near_copy = copy(near.at[pl.ds(0, ROWS)], near.at[pl.ds(ROWS, ROWS)], s_near, 0, at_grp(sibling))

    def far_copy(c):
        return copy(
            near.at[pl.ds(c * CHUNK, CHUNK)],
            far.at[pl.ds(c * WIDE, CHUNK)],
            s_far,
            c,
            at_grp(opposite),
        )

    def forward_copy(c):
        return copy(
            far.at[pl.ds(c * WIDE, CHUNK)],
            far.at[pl.ds(c * WIDE + CHUNK, CHUNK)],
            s_fwd,
            c,
            at_grp(sibling),
        )

    def far_dir_copy(c):
        rows = pl.ds(c * CHUNK, CHUNK)
        return copy(far_out.at[rows], far_in.at[rows], s_fdir, c, at_grp(sibling))

    def back_copy(c):
        rows = pl.ds(c * CHUNK, CHUNK)
        return copy(back_out.at[rows], back_in.at[rows], s_back, c, at_grp(opposite))

    def pass_on(src, dst, start, sems):
        whole = copy(
            src.at[pl.ds(0, ROWS)], dst.at[pl.ds(start, ROWS)], sems, 0, at_blk(ahead)
        )

        @pl.when(is_last)
        def _():
            slot = relay.at[0] if sems is s_text else relay.at[2]
            for j in range(RELAYS):
                pltpu.make_async_remote_copy(
                    src_ref=src.at[pl.ds(j * PIECE, PIECE)],
                    dst_ref=slot,
                    send_sem=sems.at[0, 0],
                    recv_sem=s_relay.at[1, 0 if sems is s_text else 2],
                    device_id=at_blk(base + relay_place(j)),
                    device_id_type=MESH,
                ).start()

        @pl.when(jnp.logical_not(is_last))
        def _():
            whole.start()

        return whole

    def relay_hop(k):
        return pltpu.make_async_remote_copy(
            src_ref=relay.at[k],
            dst_ref=relay.at[k + 1],
            send_sem=s_relay.at[0, k],
            recv_sem=s_relay.at[1, k + 1],
            device_id=at_blk(next_base + place),
            device_id_type=MESH,
        )

    def relay_drop(k, dst, start, sems):
        return pltpu.make_async_remote_copy(
            src_ref=relay.at[k + 1],
            dst_ref=dst.at[pl.ds(pl.multiple_of(start + piece * PIECE, PIECE), PIECE)],
            send_sem=s_relay.at[0, k + 1],
            recv_sem=sems.at[1, 0],
            device_id=at_blk(base),
            device_id_type=MESH,
        )

    def relay_first(k):
        @pl.when(is_relay)
        def _():
            copy(relay.at[k], relay.at[k], s_relay, k, at_blk(ahead)).wait_recv()
            relay_hop(k).start()

    def relay_second(k, dst, start, sems):
        @pl.when(is_relay)
        def _():
            copy(relay.at[k], relay.at[k + 1], s_relay, k + 1, at_blk(ahead)).wait_recv()
            relay_drop(k, dst, start, sems).start()

    def unit(values):
        scale = lax.rsqrt(jnp.sum(values * values, axis=-1, keepdims=True) + EPS)
        return values * scale, scale

    def image_rows(c):
        rows = pl.ds(c * CHUNK, CHUNK)
        normed, scale = unit(images_ref[rows, :].astype(jnp.float32))
        near[rows, :] = normed.astype(jnp.bfloat16)
        inverse[rows, :] = jnp.broadcast_to(scale, (CHUNK, 128))

    def text_rows(c):
        rows = pl.ds(c * CHUNK, CHUNK)
        text[rows, :] = unit(texts_ref[rows, :].astype(jnp.float32))[0].astype(jnp.bfloat16)

    loads[0].wait()
    image_rows(0)
    loads[1].wait()
    for c in range(CHUNKS):
        text_rows(c)
    pl.semaphore_wait(barrier, jnp.where(is_last, 3 + RELAYS, jnp.where(is_relay, 6, 4)))
    far_copy(0).start()
    text_copy = pass_on(text, text, ROWS, s_text)
    loads[2].wait()
    for c in range(1, CHUNKS):
        image_rows(c)

        @pl.when(jnp.logical_not(is_relay))
        def _():
            far_copy(c).start()

    near_copy.start()
    loads[3].wait()

    sharp = jnp.exp(jnp.full((8, 128), sharp_ref[0], jnp.float32))
    sharp_row = sharp[0:1, :]
    bias = bias_ref[0]

    def pair_terms(products, weights, positive=None):
        logits = sharp_row * products + bias
        decay = jnp.exp(-jnp.abs(logits))
        share = jnp.where(logits >= 0, 1.0, decay) / (1.0 + decay)
        signed = logits
        if positive is not None:
            signed = jnp.where(positive, -logits, logits)
            share = jnp.where(positive, share - 1.0, share)
        losses = jnp.maximum(signed, 0.0) + jnp.log1p(decay)
        return jnp.sum(losses, axis=0, keepdims=True), (weights * share).astype(jnp.bfloat16)

    def against(some_text, some_images):
        return lax.dot_general(
            some_text, some_images, (((1,), (1,)), ((), ())), preferred_element_type=jnp.float32
        )

    def toward(some_grads, some_text):
        return lax.dot_general(
            some_grads, some_text, (((0,), (0,)), ((), ())), preferred_element_type=jnp.float32
        )

    def near_step(k, visit):
        slot, half = k // 2, k % 2
        owner = member if slot == 0 else sibling
        rows = pl.ds(k * WIDE, WIDE)
        texts_at = pl.ds(visit * ROWS, ROWS)
        weights = weight_ref[pl.ds(2 * owner + half, 1), :]
        positive = None
        if visit == 0 and slot == 0:
            shape = (ROWS, WIDE)
            positive = lax.broadcasted_iota(jnp.int32, shape, 0) == (
                lax.broadcasted_iota(jnp.int32, shape, 1) + half * WIDE
            )
        losses, grads = pair_terms(against(text[texts_at, :], near[rows, :]), weights, positive)
        grads_near[texts_at, rows] = grads
        if visit == 0:
            loss_out[slot, pl.ds(half, 1), :] = losses
        else:
            loss_out[slot, pl.ds(half, 1), :] += losses

    def near_dir(k):
        slot, half = k // 2, k % 2
        total = toward(grads_near[:, pl.ds(k * WIDE, WIDE)], text[...])
        rows = pl.ds(half * WIDE, WIDE)
        if slot == 0:
            own_dir[rows, :] = total
        else:
            near_out[rows, :] = total.astype(jnp.bfloat16)

    left = lax.broadcasted_iota(jnp.int32, (1, WIDE), 1) < CHUNK
    swap = lambda row: pltpu.roll(row, CHUNK, 1)

    def far_step(c, visits):
        rows = pl.ds(c * WIDE, WIDE)
        texts_at = pl.ds(visits[0] * ROWS, len(visits) * ROWS)
        one = weight_ref[pl.ds(2 * opposite + c // 2, 1), :]
        two = weight_ref[pl.ds(2 * diagonal + c // 2, 1), :]
        weights = jnp.where(left, one, swap(two)) if c % 2 == 0 else jnp.where(left, swap(one), two)
        losses, grads = pair_terms(against(text[texts_at, :], far[rows, :]), weights)
        grads_far[texts_at, rows] = grads
        if visits[0] == 0:
            far_loss[c, pl.ds(0, 1), :] = losses
        else:
            far_loss[c, pl.ds(0, 1), :] += losses

    def far_dir(c):
        total = toward(grads_far[:, pl.ds(c * WIDE, WIDE)], text[...])
        far_out[pl.ds(c * CHUNK, CHUNK), :] = total[CHUNK:].astype(jnp.bfloat16)
        far_dir_copy(c).start()
        return total[:CHUNK]

    def far_arrives(c):
        far_copy(c).wait_recv()
        forward_copy(c).start()
        forward_copy(c).wait_recv()

    def far_sum(c, mine):
        far_dir_copy(c).wait_recv()
        rows = pl.ds(c * CHUNK, CHUNK)
        back_out[rows, :] = (mine + far_in[rows, :].astype(jnp.float32)).astype(jnp.bfloat16)

    def text_near(visit):
        texts_at = pl.ds(visit * ROWS, ROWS)
        text_sum[texts_at, :] = jnp.dot(
            grads_near[texts_at, :], near[...], preferred_element_type=jnp.float32
        )

    def text_total(visit):
        texts_at = pl.ds(visit * ROWS, ROWS)
        return sharp[0:1, 0:1] * (
            text_sum[texts_at, :]
            + jnp.dot(grads_far[texts_at, :], far[...], preferred_element_type=jnp.float32)
        )

    near_step(0, 0)
    relay_first(0)

    @pl.when(is_relay)
    def _():
        for c in range(1, CHUNKS):
            far_copy(c).start()

    near_step(1, 0)
    near_copy.wait_recv()
    relay_second(0, text, ROWS, s_text)
    near_step(2, 0)
    near_step(3, 0)

    near_dir_copy = copy(near_out, near_in, s_ndir, 0, at_grp(sibling))
    for c in range(CHUNKS):
        far_arrives(c)
        if c == 0:
            far_step(c, (0,))
            text_near(0)
            text_copy.wait_recv()
            far_step(c, (1,))
        else:
            far_step(c, (0, 1))
        mine = far_dir(c)
        if c == 0:
            near_step(0, 1)
            near_step(1, 1)
        if c == 1:
            near_step(2, 1)
            near_step(3, 1)
        if c == 2:
            near_dir(2)
            near_dir(3)
            near_dir_copy.start()
        far_sum(c, mine)
        if c < HELD:
            back_copy(c).start()
        else:

            @pl.when(jnp.logical_not(is_relay))
            def _():
                back_copy(c).start()

    carry_out[...] = text_total(0).astype(jnp.bfloat16)
    carry_copy = pass_on(carry_out, carry_in, 0, s_carry)
    near_dir(0)
    near_dir(1)
    text_near(1)

    for half in range(2):
        even, odd = far_loss[2 * half, 0:1, :], far_loss[2 * half + 1, 0:1, :]
        loss_out[2, pl.ds(half, 1), :] = jnp.where(left, even, swap(odd))
        loss_out[3, pl.ds(half, 1), :] = jnp.where(left, swap(even), odd)
    loss_copies = [
        copy(loss_out.at[k + 1], loss_in.at[k], s_loss, k, at_grp(other))
        for k, other in enumerate((sibling, opposite, diagonal))
    ]
    for one in loss_copies:
        one.start()

    relay_first(2)

    @pl.when(is_relay)
    def _():
        for c in range(HELD, CHUNKS):
            back_copy(c).start()

    text_sum[pl.ds(ROWS, ROWS), :] = text_total(1)
    relay_second(2, carry_in, 0, s_carry)
    carry_copy.wait_recv()
    text_grad_ref[...] = (text_sum[pl.ds(ROWS, ROWS), :] + carry_in[...].astype(jnp.float32)).astype(
        jnp.bfloat16
    )

    for one in loss_copies:
        one.wait_recv()
    total_loss = loss_out[0] + loss_in[0] + loss_in[1] + loss_in[2]
    row_loss_ref[...] = total_loss[0:2, :] / (STEPS * 4 * ROWS)

    near_dir_copy.wait_recv()
    for c in range(CHUNKS):
        rows = pl.ds(c * CHUNK, CHUNK)
        back_copy(c).wait_recv()
        step = sharp[0:1, 0:1] * (
            own_dir[rows, :]
            + near_in[rows, :].astype(jnp.float32)
            + back_in[rows, :].astype(jnp.float32)
        )
        scale = inverse[rows, 0:1]
        normed = images_ref[rows, :].astype(jnp.float32) * scale
        image_grad_ref[rows, :] = scale * (
            step - normed * jnp.sum(normed * step, axis=-1, keepdims=True)
        )

    near_copy.wait_send()
    text_copy.wait_send()
    near_dir_copy.wait_send()
    carry_copy.wait_send()
    for one in loss_copies:
        one.wait_send()
    for c in range(CHUNKS):
        far_copy(c).wait_send()
        forward_copy(c).wait_send()
        far_dir_copy(c).wait_send()
        back_copy(c).wait_send()

    @pl.when(is_relay)
    def _():
        for k, dst, start, sems in ((0, text, ROWS, s_text), (2, carry_in, 0, s_carry)):
            relay_hop(k).wait_send()
            relay_drop(k, dst, start, sems).wait_send()


def local(images, texts, row_weight, log_sharpness_parameter, bias):
    rows, features = images.shape
    vmem = pl.BlockSpec(memory_space=pltpu.VMEM)
    smem = pl.BlockSpec(memory_space=pltpu.SMEM)
    hbm = pl.BlockSpec(memory_space=pltpu.HBM)
    half = lambda n: pltpu.VMEM((n, features), jnp.bfloat16)
    sems = lambda n: pltpu.SemaphoreType.DMA((2, n))
    image_grad, text_grad, row_loss = pl.pallas_call(
        functools.partial(kernel, features),
        out_shape=(
            jax.ShapeDtypeStruct((rows, features), jnp.float32),
            jax.ShapeDtypeStruct((rows, features), jnp.bfloat16),
            jax.ShapeDtypeStruct((2, 128), jnp.float32),
        ),
        in_specs=[smem, smem, hbm, hbm, hbm],
        out_specs=(vmem, vmem, vmem),
        scratch_shapes=[
            half(ROWS),
            half(ROWS),
            pltpu.VMEM((8, 128), jnp.float32),
            half(2 * ROWS),
            half(2 * ROWS),
            half(2 * ROWS),
            pltpu.VMEM((2 * ROWS, 2 * ROWS), jnp.bfloat16),
            pltpu.VMEM((2 * ROWS, 2 * ROWS), jnp.bfloat16),
            pltpu.VMEM((ROWS, 128), jnp.float32),
            pltpu.VMEM((ROWS, features), jnp.float32),
            half(ROWS),
            half(ROWS),
            half(ROWS),
            half(ROWS),
            half(ROWS),
            half(ROWS),
            half(ROWS),
            half(ROWS),
            pltpu.VMEM((4, PIECE, features), jnp.bfloat16),
            pltpu.VMEM((4, 8, 128), jnp.float32),
            pltpu.VMEM((3, 8, 128), jnp.float32),
            pltpu.VMEM((CHUNKS, 8, 128), jnp.float32),
            pltpu.VMEM((2 * ROWS, features), jnp.float32),
            sems(1),
            sems(CHUNKS),
            sems(1),
            sems(CHUNKS),
            sems(1),
            sems(CHUNKS),
            sems(CHUNKS),
            sems(1),
            sems(3),
            sems(4),
            pltpu.SemaphoreType.DMA((4,)),
        ],
        compiler_params=pltpu.CompilerParams(
            collective_id=0, has_side_effects=True, vmem_limit_bytes=48 << 20
        ),
        name="pairs",
    )(log_sharpness_parameter, bias, row_weight.reshape(8, 128), images, texts)
    return (image_grad, text_grad, row_loss.reshape(rows))


def solution(mesh):
    placed = (P(("blk", "grp"), None), P(("blk", "grp"), None), P("blk"), P(), P())
    return jax.shard_map(
        local,
        mesh=mesh,
        in_specs=placed,
        out_specs=(P(("blk", "grp"), None), P(("blk", "grp"), None), P(("blk", "grp"))),
        check_vma=False,
    )
```

```python
import functools

import jax
import jax.numpy as jnp
from jax import lax
from jax.experimental import pallas as pl
from jax.experimental.pallas import tpu as pltpu
from jax.sharding import PartitionSpec as P

MESH = pl.DeviceIdType.MESH
STEPS = 2
ROWS = 256
CHUNK = 64
CHUNKS = ROWS // CHUNK
WIDE = 128
PLANE = 48
RELAYS = ((44, True), (45, True), (46, True)) + tuple((p, False) for p in (40, 36, 33, 4, 3))
PIECE = ROWS // len(RELAYS)
EPS = 1e-06


def kernel(
    features,
    sharp_ref,
    bias_ref,
    weights_hbm,
    images_hbm,
    texts_hbm,
    image_grad_ref,
    text_grad_ref,
    row_loss_ref,
    images_ref,
    texts_ref,
    weight_ref,
    near,
    far,
    text,
    grads_near,
    grads_far,
    inverse,
    own_dir,
    near_out,
    near_in,
    far_out,
    far_in,
    back_out,
    back_in,
    carry_out,
    carry_in,
    relay,
    loss_out,
    loss_in,
    far_loss,
    text_sum,
    s_near,
    s_far,
    s_text,
    s_fwd,
    s_ndir,
    s_fdir,
    s_back,
    s_carry,
    s_loss,
    s_relay,
    s_load,
):
    loads = [
        pltpu.make_async_copy(
            images_hbm.at[pl.ds(0, CHUNK)], images_ref.at[pl.ds(0, CHUNK)], s_load.at[0]
        ),
        pltpu.make_async_copy(texts_hbm, texts_ref, s_load.at[1]),
        pltpu.make_async_copy(
            images_hbm.at[pl.ds(CHUNK, ROWS - CHUNK)],
            images_ref.at[pl.ds(CHUNK, ROWS - CHUNK)],
            s_load.at[2],
        ),
        pltpu.make_async_copy(weights_hbm, weight_ref, s_load.at[3]),
    ]
    for one in loads:
        one.start()
    blk = lax.axis_index("blk")
    member = lax.axis_index("grp")
    groups = lax.axis_size("blk")
    sibling = member + 1 - 2 * lax.rem(member, 2)
    opposite = lax.rem(member + 2, 4)
    diagonal = lax.rem(sibling + 2, 4)
    at_grp = lambda g: {"blk": blk, "grp": g}
    at_blk = lambda b: {"blk": b, "grp": member}
    ahead = lax.rem(blk + 1, groups)
    behind = lax.rem(blk + groups - 1, groups)
    place = lax.rem(blk, PLANE)
    base = blk - place
    next_base = lax.rem(base + PLANE, groups)
    last_base = lax.rem(base + groups - PLANE, groups)
    is_last = place == PLANE - 1
    is_first = place == 0
    is_relay = functools.reduce(jnp.logical_or, [place == p for p, _ in RELAYS])
    piece = sum(j * (place == p).astype(jnp.int32) for j, (p, _) in enumerate(RELAYS))
    at_old = functools.reduce(jnp.logical_or, [place == p for p, old in RELAYS if old])

    def copy(src, dst, sems, k, device):
        return pltpu.make_async_remote_copy(
            src_ref=src,
            dst_ref=dst,
            send_sem=sems.at[0, k],
            recv_sem=sems.at[1, k],
            device_id=device,
            device_id_type=MESH,
        )

    barrier = pltpu.get_barrier_semaphore()

    def greet(device):
        pl.semaphore_signal(barrier, inc=1, device_id=device, device_id_type=MESH)

    for other in (sibling, opposite, diagonal):
        greet(at_grp(other))

    @pl.when(is_first)
    def _():
        for p, old in RELAYS:
            greet(at_blk((last_base if old else base) + p))

    @pl.when(jnp.logical_not(is_first))
    def _():
        greet(at_blk(behind))

    @pl.when(is_relay)
    def _():
        greet(at_blk(jnp.where(at_old, base, last_base) + PLANE - 1))

    near_copy = copy(near.at[pl.ds(0, ROWS)], near.at[pl.ds(ROWS, ROWS)], s_near, 0, at_grp(sibling))

    def far_copy(c):
        return copy(
            near.at[pl.ds(c * CHUNK, CHUNK)],
            far.at[pl.ds(c * WIDE, CHUNK)],
            s_far,
            c,
            at_grp(opposite),
        )

    def forward_copy(c):
        return copy(
            far.at[pl.ds(c * WIDE, CHUNK)],
            far.at[pl.ds(c * WIDE + CHUNK, CHUNK)],
            s_fwd,
            c,
            at_grp(sibling),
        )

    def far_dir_copy(c):
        rows = pl.ds(c * CHUNK, CHUNK)
        return copy(far_out.at[rows], far_in.at[rows], s_fdir, c, at_grp(sibling))

    def back_copy(c):
        rows = pl.ds(c * CHUNK, CHUNK)
        return copy(back_out.at[rows], back_in.at[rows], s_back, c, at_grp(opposite))

    def pass_on(src, dst, start, sems):
        whole = copy(
            src.at[pl.ds(0, ROWS)], dst.at[pl.ds(start, ROWS)], sems, 0, at_blk(ahead)
        )

        @pl.when(is_last)
        def _():
            k = 0 if sems is s_text else 1
            for j, (p, old) in enumerate(RELAYS):
                pltpu.make_async_remote_copy(
                    src_ref=src.at[pl.ds(j * PIECE, PIECE)],
                    dst_ref=relay.at[k],
                    send_sem=sems.at[0, 0],
                    recv_sem=s_relay.at[1, k],
                    device_id=at_blk((base if old else next_base) + p),
                    device_id_type=MESH,
                ).start()

        @pl.when(jnp.logical_not(is_last))
        def _():
            whole.start()

        return whole

    def relay_copy(k, dst, start, sems):
        return pltpu.make_async_remote_copy(
            src_ref=relay.at[k],
            dst_ref=dst.at[pl.ds(pl.multiple_of(start + piece * PIECE, PIECE), PIECE)],
            send_sem=s_relay.at[0, k],
            recv_sem=sems.at[1, 0],
            device_id=at_blk(jnp.where(at_old, next_base, base)),
            device_id_type=MESH,
        )

    def relay_on(k, dst, start, sems):
        @pl.when(is_relay)
        def _():
            copy(relay.at[k], relay.at[k], s_relay, k, at_blk(ahead)).wait_recv()
            relay_copy(k, dst, start, sems).start()

    def unit(values):
        scale = lax.rsqrt(jnp.sum(values * values, axis=-1, keepdims=True) + EPS)
        return values * scale, scale

    def image_rows(c):
        rows = pl.ds(c * CHUNK, CHUNK)
        normed, scale = unit(images_ref[rows, :].astype(jnp.float32))
        near[rows, :] = normed.astype(jnp.bfloat16)
        inverse[rows, :] = jnp.broadcast_to(scale, (CHUNK, 128))

    def text_rows(c):
        rows = pl.ds(c * CHUNK, CHUNK)
        text[rows, :] = unit(texts_ref[rows, :].astype(jnp.float32))[0].astype(jnp.bfloat16)

    loads[0].wait()
    image_rows(0)
    loads[1].wait()
    for c in range(CHUNKS):
        text_rows(c)
    pl.semaphore_wait(barrier, jnp.where(is_last, 3 + len(RELAYS), jnp.where(is_relay, 5, 4)))
    far_copy(0).start()
    text_copy = pass_on(text, text, ROWS, s_text)
    loads[2].wait()
    for c in range(1, CHUNKS):
        image_rows(c)
        far_copy(c).start()

    near_copy.start()
    loads[3].wait()

    sharp = jnp.exp(jnp.full((8, 128), sharp_ref[0], jnp.float32))
    sharp_row = sharp[0:1, :]
    bias = bias_ref[0]

    def pair_terms(products, weights, positive=None):
        logits = sharp_row * products + bias
        decay = jnp.exp(-jnp.abs(logits))
        share = jnp.where(logits >= 0, 1.0, decay) / (1.0 + decay)
        signed = logits
        if positive is not None:
            signed = jnp.where(positive, -logits, logits)
            share = jnp.where(positive, share - 1.0, share)
        losses = jnp.maximum(signed, 0.0) + jnp.log1p(decay)
        return jnp.sum(losses, axis=0, keepdims=True), (weights * share).astype(jnp.bfloat16)

    def against(some_text, some_images):
        return lax.dot_general(
            some_text, some_images, (((1,), (1,)), ((), ())), preferred_element_type=jnp.float32
        )

    def toward(some_grads, some_text):
        return lax.dot_general(
            some_grads, some_text, (((0,), (0,)), ((), ())), preferred_element_type=jnp.float32
        )

    def near_step(k, visit):
        slot, half = k // 2, k % 2
        owner = member if slot == 0 else sibling
        rows = pl.ds(k * WIDE, WIDE)
        texts_at = pl.ds(visit * ROWS, ROWS)
        weights = weight_ref[pl.ds(2 * owner + half, 1), :]
        positive = None
        if visit == 0 and slot == 0:
            shape = (ROWS, WIDE)
            positive = lax.broadcasted_iota(jnp.int32, shape, 0) == (
                lax.broadcasted_iota(jnp.int32, shape, 1) + half * WIDE
            )
        losses, grads = pair_terms(against(text[texts_at, :], near[rows, :]), weights, positive)
        grads_near[texts_at, rows] = grads
        if visit == 0:
            loss_out[slot, pl.ds(half, 1), :] = losses
        else:
            loss_out[slot, pl.ds(half, 1), :] += losses

    def near_dir(k):
        slot, half = k // 2, k % 2
        total = toward(grads_near[:, pl.ds(k * WIDE, WIDE)], text[...])
        rows = pl.ds(half * WIDE, WIDE)
        if slot == 0:
            own_dir[rows, :] = total
        else:
            near_out[rows, :] = total.astype(jnp.bfloat16)

    left = lax.broadcasted_iota(jnp.int32, (1, WIDE), 1) < CHUNK
    swap = lambda row: pltpu.roll(row, CHUNK, 1)

    def far_step(c, visit):
        rows = pl.ds(c * WIDE, WIDE)
        texts_at = pl.ds(visit * ROWS, ROWS)
        one = weight_ref[pl.ds(2 * opposite + c // 2, 1), :]
        two = weight_ref[pl.ds(2 * diagonal + c // 2, 1), :]
        weights = jnp.where(left, one, swap(two)) if c % 2 == 0 else jnp.where(left, swap(one), two)
        losses, grads = pair_terms(against(text[texts_at, :], far[rows, :]), weights)
        grads_far[texts_at, rows] = grads
        if visit == 0:
            far_loss[c, pl.ds(0, 1), :] = losses
        else:
            far_loss[c, pl.ds(0, 1), :] += losses

    def far_dir(c):
        total = toward(grads_far[:, pl.ds(c * WIDE, WIDE)], text[...])
        far_out[pl.ds(c * CHUNK, CHUNK), :] = total[CHUNK:].astype(jnp.bfloat16)
        far_dir_copy(c).start()
        return total[:CHUNK]

    def far_arrives(c):
        far_copy(c).wait_recv()
        forward_copy(c).start()
        forward_copy(c).wait_recv()

    def far_sum(c, mine):
        far_dir_copy(c).wait_recv()
        rows = pl.ds(c * CHUNK, CHUNK)
        back_out[rows, :] = (mine + far_in[rows, :].astype(jnp.float32)).astype(jnp.bfloat16)

    def text_near(visit):
        texts_at = pl.ds(visit * ROWS, ROWS)
        text_sum[texts_at, :] = jnp.dot(
            grads_near[texts_at, :], near[...], preferred_element_type=jnp.float32
        )

    def text_total(visit):
        texts_at = pl.ds(visit * ROWS, ROWS)
        return sharp[0:1, 0:1] * (
            text_sum[texts_at, :]
            + jnp.dot(grads_far[texts_at, :], far[...], preferred_element_type=jnp.float32)
        )

    near_step(0, 0)
    near_step(1, 0)
    near_copy.wait_recv()
    near_step(2, 0)
    near_step(3, 0)
    relay_on(0, text, ROWS, s_text)

    near_dir_copy = copy(near_out, near_in, s_ndir, 0, at_grp(sibling))
    for c in range(2):
        far_arrives(c)
        far_step(c, 0)
    text_near(0)

    @pl.when(is_first)
    def _():
        for c in range(2, CHUNKS):
            far_arrives(c)
            far_step(c, 0)

    text_copy.wait_recv()
    for c in range(CHUNKS):
        if c >= 2:

            @pl.when(jnp.logical_not(is_first))
            def _():
                far_arrives(c)
                far_step(c, 0)

        far_step(c, 1)
        mine = far_dir(c)
        if c < 2:
            near_step(2 * c, 1)
            near_step(2 * c + 1, 1)
        if c == 2:
            near_dir(2)
            near_dir(3)
            near_dir_copy.start()
        if c == 3:
            near_dir(0)
            near_dir(1)
        far_sum(c, mine)
        back_copy(c).start()

    carry_out[...] = text_total(0).astype(jnp.bfloat16)
    carry_copy = pass_on(carry_out, carry_in, 0, s_carry)
    text_near(1)

    for half in range(2):
        even, odd = far_loss[2 * half, 0:1, :], far_loss[2 * half + 1, 0:1, :]
        loss_out[2, pl.ds(half, 1), :] = jnp.where(left, even, swap(odd))
        loss_out[3, pl.ds(half, 1), :] = jnp.where(left, swap(even), odd)
    loss_copies = [
        copy(loss_out.at[k + 1], loss_in.at[k], s_loss, k, at_grp(other))
        for k, other in enumerate((sibling, opposite, diagonal))
    ]
    for one in loss_copies:
        one.start()

    text_sum[pl.ds(ROWS, ROWS), :] = text_total(1)
    relay_on(1, carry_in, 0, s_carry)
    carry_copy.wait_recv()
    text_grad_ref[...] = (text_sum[pl.ds(ROWS, ROWS), :] + carry_in[...].astype(jnp.float32)).astype(
        jnp.bfloat16
    )

    for one in loss_copies:
        one.wait_recv()
    total_loss = loss_out[0] + loss_in[0] + loss_in[1] + loss_in[2]
    row_loss_ref[...] = total_loss[0:2, :] / (STEPS * 4 * ROWS)

    near_dir_copy.wait_recv()
    for c in range(CHUNKS):
        rows = pl.ds(c * CHUNK, CHUNK)
        back_copy(c).wait_recv()
        step = sharp[0:1, 0:1] * (
            own_dir[rows, :]
            + near_in[rows, :].astype(jnp.float32)
            + back_in[rows, :].astype(jnp.float32)
        )
        scale = inverse[rows, 0:1]
        normed = images_ref[rows, :].astype(jnp.float32) * scale
        image_grad_ref[rows, :] = scale * (
            step - normed * jnp.sum(normed * step, axis=-1, keepdims=True)
        )

    near_copy.wait_send()
    text_copy.wait_send()
    near_dir_copy.wait_send()
    carry_copy.wait_send()
    for one in loss_copies:
        one.wait_send()
    for c in range(CHUNKS):
        far_copy(c).wait_send()
        forward_copy(c).wait_send()
        far_dir_copy(c).wait_send()
        back_copy(c).wait_send()

    @pl.when(is_relay)
    def _():
        relay_copy(0, text, ROWS, s_text).wait_send()
        relay_copy(1, carry_in, 0, s_carry).wait_send()


def local(images, texts, row_weight, log_sharpness_parameter, bias):
    rows, features = images.shape
    vmem = pl.BlockSpec(memory_space=pltpu.VMEM)
    smem = pl.BlockSpec(memory_space=pltpu.SMEM)
    hbm = pl.BlockSpec(memory_space=pltpu.HBM)
    half = lambda n: pltpu.VMEM((n, features), jnp.bfloat16)
    sems = lambda n: pltpu.SemaphoreType.DMA((2, n))
    stay = [
        pltpu.with_memory_space_constraint(value, pltpu.HBM)
        for value in (row_weight.reshape(8, 128), images, texts)
    ]
    image_grad, text_grad, row_loss = pl.pallas_call(
        functools.partial(kernel, features),
        out_shape=(
            jax.ShapeDtypeStruct((rows, features), jnp.float32),
            jax.ShapeDtypeStruct((rows, features), jnp.bfloat16),
            jax.ShapeDtypeStruct((2, 128), jnp.float32),
        ),
        in_specs=[smem, smem, hbm, hbm, hbm],
        out_specs=(vmem, vmem, vmem),
        scratch_shapes=[
            half(ROWS),
            half(ROWS),
            pltpu.VMEM((8, 128), jnp.float32),
            half(2 * ROWS),
            half(2 * ROWS),
            half(2 * ROWS),
            pltpu.VMEM((2 * ROWS, 2 * ROWS), jnp.bfloat16),
            pltpu.VMEM((2 * ROWS, 2 * ROWS), jnp.bfloat16),
            pltpu.VMEM((ROWS, 128), jnp.float32),
            pltpu.VMEM((ROWS, features), jnp.float32),
            half(ROWS),
            half(ROWS),
            half(ROWS),
            half(ROWS),
            half(ROWS),
            half(ROWS),
            half(ROWS),
            half(ROWS),
            pltpu.VMEM((2, PIECE, features), jnp.bfloat16),
            pltpu.VMEM((4, 8, 128), jnp.float32),
            pltpu.VMEM((3, 8, 128), jnp.float32),
            pltpu.VMEM((CHUNKS, 8, 128), jnp.float32),
            pltpu.VMEM((2 * ROWS, features), jnp.float32),
            sems(1),
            sems(CHUNKS),
            sems(1),
            sems(CHUNKS),
            sems(1),
            sems(CHUNKS),
            sems(CHUNKS),
            sems(1),
            sems(3),
            sems(2),
            pltpu.SemaphoreType.DMA((4,)),
        ],
        compiler_params=pltpu.CompilerParams(
            collective_id=0, has_side_effects=True, vmem_limit_bytes=48 << 20
        ),
        name="pairs",
    )(log_sharpness_parameter, bias, *stay)
    return (image_grad, text_grad, row_loss.reshape(rows))


def solution(mesh):
    placed = (P(("blk", "grp"), None), P(("blk", "grp"), None), P("blk"), P(), P())
    return jax.shard_map(
        local,
        mesh=mesh,
        in_specs=placed,
        out_specs=(P(("blk", "grp"), None), P(("blk", "grp"), None), P(("blk", "grp"))),
        check_vma=False,
    )
```

```python
import functools

import jax
import jax.numpy as jnp
from jax import lax
from jax.experimental import pallas as pl
from jax.experimental.pallas import tpu as pltpu
from jax.sharding import PartitionSpec as P

MESH = pl.DeviceIdType.MESH
STEPS = 2
ROWS = 256
CHUNK = 64
CHUNKS = ROWS // CHUNK
WIDE = 128
PLANE = 48
RELAYS = ((45, True), (46, True)) + tuple((p, False) for p in (40, 36, 33, 8, 4, 3))
PIECE = ROWS // len(RELAYS)
EPS = 1e-06


def kernel(
    features,
    sharp_ref,
    bias_ref,
    weights_hbm,
    images_hbm,
    texts_hbm,
    image_grad_ref,
    text_grad_ref,
    row_loss_ref,
    images_ref,
    texts_ref,
    weight_ref,
    near,
    far,
    text,
    grads_near,
    grads_far,
    inverse,
    own_dir,
    near_out,
    near_in,
    far_out,
    far_in,
    back_out,
    back_in,
    carry_out,
    carry_in,
    relay,
    loss_out,
    loss_in,
    far_loss,
    text_sum,
    s_near,
    s_far,
    s_text,
    s_fwd,
    s_ndir,
    s_fdir,
    s_back,
    s_carry,
    s_loss,
    s_relay,
    s_load,
):
    loads = [
        pltpu.make_async_copy(
            images_hbm.at[pl.ds(0, CHUNK)], images_ref.at[pl.ds(0, CHUNK)], s_load.at[0]
        ),
        pltpu.make_async_copy(texts_hbm, texts_ref.at[pl.ds(0, ROWS)], s_load.at[1]),
        pltpu.make_async_copy(
            images_hbm.at[pl.ds(CHUNK, ROWS - CHUNK)],
            images_ref.at[pl.ds(CHUNK, ROWS - CHUNK)],
            s_load.at[2],
        ),
        pltpu.make_async_copy(weights_hbm, weight_ref, s_load.at[3]),
    ]
    for one in loads:
        one.start()
    blk = lax.axis_index("blk")
    member = lax.axis_index("grp")
    groups = lax.axis_size("blk")
    sibling = member + 1 - 2 * lax.rem(member, 2)
    opposite = lax.rem(member + 2, 4)
    diagonal = lax.rem(sibling + 2, 4)
    at_grp = lambda g: {"blk": blk, "grp": g}
    at_blk = lambda b: {"blk": b, "grp": member}
    ahead = lax.rem(blk + 1, groups)
    behind = lax.rem(blk + groups - 1, groups)
    place = lax.rem(blk, PLANE)
    base = blk - place
    next_base = lax.rem(base + PLANE, groups)
    last_base = lax.rem(base + groups - PLANE, groups)
    is_last = place == PLANE - 1
    is_first = place == 0
    is_relay = functools.reduce(jnp.logical_or, [place == p for p, _ in RELAYS])
    piece = sum(j * (place == p).astype(jnp.int32) for j, (p, _) in enumerate(RELAYS))
    at_old = functools.reduce(jnp.logical_or, [place == p for p, old in RELAYS if old])

    def copy(src, dst, sems, k, device):
        return pltpu.make_async_remote_copy(
            src_ref=src,
            dst_ref=dst,
            send_sem=sems.at[0, k],
            recv_sem=sems.at[1, k],
            device_id=device,
            device_id_type=MESH,
        )

    barrier = pltpu.get_barrier_semaphore()

    def greet(device):
        pl.semaphore_signal(barrier, inc=1, device_id=device, device_id_type=MESH)

    for other in (sibling, opposite, diagonal):
        greet(at_grp(other))

    @pl.when(is_first)
    def _():
        for p, old in RELAYS:
            greet(at_blk((last_base if old else base) + p))

    @pl.when(jnp.logical_not(is_first))
    def _():
        greet(at_blk(behind))

    @pl.when(is_relay)
    def _():
        greet(at_blk(jnp.where(at_old, base, last_base) + PLANE - 1))

    near_copy = copy(near.at[pl.ds(0, ROWS)], near.at[pl.ds(ROWS, ROWS)], s_near, 0, at_grp(sibling))

    def far_copy(c):
        return copy(
            near.at[pl.ds(c * CHUNK, CHUNK)],
            far.at[pl.ds(c * WIDE, CHUNK)],
            s_far,
            c,
            at_grp(opposite),
        )

    def forward_copy(c):
        return copy(
            far.at[pl.ds(c * WIDE, CHUNK)],
            far.at[pl.ds(c * WIDE + CHUNK, CHUNK)],
            s_fwd,
            c,
            at_grp(sibling),
        )

    def far_dir_copy(c):
        rows = pl.ds(c * CHUNK, CHUNK)
        return copy(far_out.at[rows], far_in.at[rows], s_fdir, c, at_grp(sibling))

    def back_copy(c):
        rows = pl.ds(c * CHUNK, CHUNK)
        return copy(back_out.at[rows], back_in.at[rows], s_back, c, at_grp(opposite))

    def pass_on(src, dst, start, sems):
        whole = copy(
            src.at[pl.ds(0, ROWS)], dst.at[pl.ds(start, ROWS)], sems, 0, at_blk(ahead)
        )

        @pl.when(is_last)
        def _():
            k = 0 if sems is s_text else 1
            for j, (p, old) in enumerate(RELAYS):
                pltpu.make_async_remote_copy(
                    src_ref=src.at[pl.ds(j * PIECE, PIECE)],
                    dst_ref=relay.at[k],
                    send_sem=sems.at[0, 0],
                    recv_sem=s_relay.at[1, k],
                    device_id=at_blk((base if old else next_base) + p),
                    device_id_type=MESH,
                ).start()

        @pl.when(jnp.logical_not(is_last))
        def _():
            whole.start()

        return whole

    def relay_copy(k, dst, start, sems):
        return pltpu.make_async_remote_copy(
            src_ref=relay.at[k],
            dst_ref=dst.at[pl.ds(pl.multiple_of(start + piece * PIECE, PIECE), PIECE)],
            send_sem=s_relay.at[0, k],
            recv_sem=sems.at[1, 0],
            device_id=at_blk(jnp.where(at_old, next_base, base)),
            device_id_type=MESH,
        )

    def relay_on(k, dst, start, sems):
        @pl.when(is_relay)
        def _():
            copy(relay.at[k], relay.at[k], s_relay, k, at_blk(ahead)).wait_recv()
            relay_copy(k, dst, start, sems).start()

    def unit(values):
        scale = lax.rsqrt(jnp.sum(values * values, axis=-1, keepdims=True) + EPS)
        return values * scale, scale

    def image_rows(c):
        rows = pl.ds(c * CHUNK, CHUNK)
        normed, scale = unit(images_ref[rows, :].astype(jnp.float32))
        near[rows, :] = normed.astype(jnp.bfloat16)
        inverse[rows, :] = jnp.broadcast_to(scale, (CHUNK, 128))

    def text_rows(c):
        rows = pl.ds(c * CHUNK, CHUNK)
        text[rows, :] = unit(texts_ref[rows, :].astype(jnp.float32))[0].astype(jnp.bfloat16)

    loads[0].wait()
    image_rows(0)
    pl.semaphore_wait(barrier, jnp.where(is_last, 3 + len(RELAYS), jnp.where(is_relay, 5, 4)))
    far_copy(0).start()
    text_copy = pass_on(texts_hbm, texts_ref, ROWS, s_text)
    loads[2].wait()
    for c in range(1, CHUNKS):
        image_rows(c)
        far_copy(c).start()

    near_copy.start()
    loads[1].wait()
    for c in range(CHUNKS):
        text_rows(c)
    loads[3].wait()

    sharp = jnp.exp(jnp.full((8, 128), sharp_ref[0], jnp.float32))
    sharp_row = sharp[0:1, :]
    bias = bias_ref[0]

    def pair_terms(products, weights, positive=None):
        logits = sharp_row * products + bias
        decay = jnp.exp(-jnp.abs(logits))
        share = jnp.where(logits >= 0, 1.0, decay) / (1.0 + decay)
        signed = logits
        if positive is not None:
            signed = jnp.where(positive, -logits, logits)
            share = jnp.where(positive, share - 1.0, share)
        losses = jnp.maximum(signed, 0.0) + jnp.log1p(decay)
        return jnp.sum(losses, axis=0, keepdims=True), (weights * share).astype(jnp.bfloat16)

    def against(some_text, some_images):
        return lax.dot_general(
            some_text, some_images, (((1,), (1,)), ((), ())), preferred_element_type=jnp.float32
        )

    def toward(some_grads, some_text):
        return lax.dot_general(
            some_grads, some_text, (((0,), (0,)), ((), ())), preferred_element_type=jnp.float32
        )

    def near_step(k, visit):
        slot, half = k // 2, k % 2
        owner = member if slot == 0 else sibling
        rows = pl.ds(k * WIDE, WIDE)
        texts_at = pl.ds(visit * ROWS, ROWS)
        weights = weight_ref[pl.ds(2 * owner + half, 1), :]
        positive = None
        if visit == 0 and slot == 0:
            shape = (ROWS, WIDE)
            positive = lax.broadcasted_iota(jnp.int32, shape, 0) == (
                lax.broadcasted_iota(jnp.int32, shape, 1) + half * WIDE
            )
        losses, grads = pair_terms(against(text[texts_at, :], near[rows, :]), weights, positive)
        grads_near[texts_at, rows] = grads
        if visit == 0:
            loss_out[slot, pl.ds(half, 1), :] = losses
        else:
            loss_out[slot, pl.ds(half, 1), :] += losses

    def near_dir(k):
        slot, half = k // 2, k % 2
        total = toward(grads_near[:, pl.ds(k * WIDE, WIDE)], text[...])
        rows = pl.ds(half * WIDE, WIDE)
        if slot == 0:
            own_dir[rows, :] = total
        else:
            near_out[rows, :] = total.astype(jnp.bfloat16)

    left = lax.broadcasted_iota(jnp.int32, (1, WIDE), 1) < CHUNK
    swap = lambda row: pltpu.roll(row, CHUNK, 1)

    def far_step(c, visit):
        rows = pl.ds(c * WIDE, WIDE)
        texts_at = pl.ds(visit * ROWS, ROWS)
        one = weight_ref[pl.ds(2 * opposite + c // 2, 1), :]
        two = weight_ref[pl.ds(2 * diagonal + c // 2, 1), :]
        weights = jnp.where(left, one, swap(two)) if c % 2 == 0 else jnp.where(left, swap(one), two)
        losses, grads = pair_terms(against(text[texts_at, :], far[rows, :]), weights)
        grads_far[texts_at, rows] = grads
        if visit == 0:
            far_loss[c, pl.ds(0, 1), :] = losses
        else:
            far_loss[c, pl.ds(0, 1), :] += losses

    def far_dir(c):
        total = toward(grads_far[:, pl.ds(c * WIDE, WIDE)], text[...])
        far_out[pl.ds(c * CHUNK, CHUNK), :] = total[CHUNK:].astype(jnp.bfloat16)
        far_dir_copy(c).start()
        return total[:CHUNK]

    def far_arrives(c):
        far_copy(c).wait_recv()
        forward_copy(c).start()
        forward_copy(c).wait_recv()

    def far_sum(c, mine):
        far_dir_copy(c).wait_recv()
        rows = pl.ds(c * CHUNK, CHUNK)
        back_out[rows, :] = (mine + far_in[rows, :].astype(jnp.float32)).astype(jnp.bfloat16)

    def text_near(visit):
        texts_at = pl.ds(visit * ROWS, ROWS)
        text_sum[texts_at, :] = jnp.dot(
            grads_near[texts_at, :], near[...], preferred_element_type=jnp.float32
        )

    def text_far(visit, rows):
        texts_at = pl.ds(visit * ROWS, ROWS)
        return text_sum[texts_at, :] + jnp.dot(
            grads_far[texts_at, rows], far[rows, :], preferred_element_type=jnp.float32
        )

    early, late = pl.ds(0, 3 * WIDE), pl.ds(3 * WIDE, WIDE)

    near_step(0, 0)
    near_step(1, 0)
    near_copy.wait_recv()
    near_step(2, 0)
    near_step(3, 0)
    relay_on(0, texts_ref, ROWS, s_text)

    near_dir_copy = copy(near_out, near_in, s_ndir, 0, at_grp(sibling))
    for c in range(2):
        far_arrives(c)
        far_step(c, 0)
    text_near(0)

    @pl.when(is_first)
    def _():
        for c in range(2, CHUNKS):
            far_arrives(c)
            far_step(c, 0)

    text_copy.wait_recv()
    for c in range(CHUNKS, 2 * CHUNKS):
        text_rows(c)
    for c in range(CHUNKS):
        if c >= 2:

            @pl.when(jnp.logical_not(is_first))
            def _():
                far_arrives(c)
                far_step(c, 0)

        if c == CHUNKS - 1:
            carry_out[...] = (sharp[0:1, 0:1] * text_far(0, late)).astype(jnp.bfloat16)
            carry_copy = pass_on(carry_out, carry_in, 0, s_carry)
        far_step(c, 1)
        mine = far_dir(c)
        if c < 2:
            near_step(2 * c, 1)
            near_step(2 * c + 1, 1)
        if c == 2:
            near_dir(2)
            near_dir(3)
            near_dir_copy.start()
            text_sum[pl.ds(0, ROWS), :] = text_far(0, early)
        if c == 3:
            near_dir(0)
            near_dir(1)
        far_sum(c, mine)
        back_copy(c).start()

    for half in range(2):
        even, odd = far_loss[2 * half, 0:1, :], far_loss[2 * half + 1, 0:1, :]
        loss_out[2, pl.ds(half, 1), :] = jnp.where(left, even, swap(odd))
        loss_out[3, pl.ds(half, 1), :] = jnp.where(left, swap(even), odd)
    loss_copies = [
        copy(loss_out.at[k + 1], loss_in.at[k], s_loss, k, at_grp(other))
        for k, other in enumerate((sibling, opposite, diagonal))
    ]
    for one in loss_copies:
        one.start()

    text_near(1)
    text_sum[pl.ds(ROWS, ROWS), :] = sharp[0:1, 0:1] * text_far(1, pl.ds(0, 2 * ROWS))
    relay_on(1, carry_in, 0, s_carry)

    for one in loss_copies:
        one.wait_recv()
    total_loss = loss_out[0] + loss_in[0] + loss_in[1] + loss_in[2]
    row_loss_ref[...] = total_loss[0:2, :] / (STEPS * 4 * ROWS)

    near_dir_copy.wait_recv()
    for c in range(CHUNKS):
        rows = pl.ds(c * CHUNK, CHUNK)
        if c == CHUNKS - 1:
            carry_copy.wait_recv()
            text_grad_ref[...] = (
                text_sum[pl.ds(ROWS, ROWS), :] + carry_in[...].astype(jnp.float32)
            ).astype(jnp.bfloat16)
        back_copy(c).wait_recv()
        step = sharp[0:1, 0:1] * (
            own_dir[rows, :]
            + near_in[rows, :].astype(jnp.float32)
            + back_in[rows, :].astype(jnp.float32)
        )
        scale = inverse[rows, 0:1]
        normed = images_ref[rows, :].astype(jnp.float32) * scale
        image_grad_ref[rows, :] = scale * (
            step - normed * jnp.sum(normed * step, axis=-1, keepdims=True)
        )

    near_copy.wait_send()
    text_copy.wait_send()
    near_dir_copy.wait_send()
    carry_copy.wait_send()
    for one in loss_copies:
        one.wait_send()
    for c in range(CHUNKS):
        far_copy(c).wait_send()
        forward_copy(c).wait_send()
        far_dir_copy(c).wait_send()
        back_copy(c).wait_send()

    @pl.when(is_relay)
    def _():
        relay_copy(0, texts_ref, ROWS, s_text).wait_send()
        relay_copy(1, carry_in, 0, s_carry).wait_send()


def local(images, texts, row_weight, log_sharpness_parameter, bias):
    rows, features = images.shape
    vmem = pl.BlockSpec(memory_space=pltpu.VMEM)
    smem = pl.BlockSpec(memory_space=pltpu.SMEM)
    hbm = pl.BlockSpec(memory_space=pltpu.HBM)
    half = lambda n: pltpu.VMEM((n, features), jnp.bfloat16)
    sems = lambda n: pltpu.SemaphoreType.DMA((2, n))
    stay = [
        pltpu.with_memory_space_constraint(value, pltpu.HBM)
        for value in (row_weight.reshape(8, 128), images, texts)
    ]
    image_grad, text_grad, row_loss = pl.pallas_call(
        functools.partial(kernel, features),
        out_shape=(
            jax.ShapeDtypeStruct((rows, features), jnp.float32),
            jax.ShapeDtypeStruct((rows, features), jnp.bfloat16),
            jax.ShapeDtypeStruct((2, 128), jnp.float32),
        ),
        in_specs=[smem, smem, hbm, hbm, hbm],
        out_specs=(vmem, vmem, vmem),
        scratch_shapes=[
            half(ROWS),
            half(2 * ROWS),
            pltpu.VMEM((8, 128), jnp.float32),
            half(2 * ROWS),
            half(2 * ROWS),
            half(2 * ROWS),
            pltpu.VMEM((2 * ROWS, 2 * ROWS), jnp.bfloat16),
            pltpu.VMEM((2 * ROWS, 2 * ROWS), jnp.bfloat16),
            pltpu.VMEM((ROWS, 128), jnp.float32),
            pltpu.VMEM((ROWS, features), jnp.float32),
            half(ROWS),
            half(ROWS),
            half(ROWS),
            half(ROWS),
            half(ROWS),
            half(ROWS),
            half(ROWS),
            half(ROWS),
            pltpu.VMEM((2, PIECE, features), jnp.bfloat16),
            pltpu.VMEM((4, 8, 128), jnp.float32),
            pltpu.VMEM((3, 8, 128), jnp.float32),
            pltpu.VMEM((CHUNKS, 8, 128), jnp.float32),
            pltpu.VMEM((2 * ROWS, features), jnp.float32),
            sems(1),
            sems(CHUNKS),
            sems(1),
            sems(CHUNKS),
            sems(1),
            sems(CHUNKS),
            sems(CHUNKS),
            sems(1),
            sems(3),
            sems(2),
            pltpu.SemaphoreType.DMA((4,)),
        ],
        compiler_params=pltpu.CompilerParams(
            collective_id=0, has_side_effects=True, vmem_limit_bytes=48 << 20
        ),
        name="pairs",
    )(log_sharpness_parameter, bias, *stay)
    return (image_grad, text_grad, row_loss.reshape(rows))


def solution(mesh):
    placed = (P(("blk", "grp"), None), P(("blk", "grp"), None), P("blk"), P(), P())
    return jax.shard_map(
        local,
        mesh=mesh,
        in_specs=placed,
        out_specs=(P(("blk", "grp"), None), P(("blk", "grp"), None), P(("blk", "grp"))),
        check_vma=False,
    )
```

```python
import functools

import jax
import jax.numpy as jnp
from jax import lax
from jax.experimental import pallas as pl
from jax.experimental.pallas import tpu as pltpu
from jax.sharding import PartitionSpec as P

MESH = pl.DeviceIdType.MESH
STEPS = 2
ROWS = 256
CHUNK = 64
CHUNKS = ROWS // CHUNK
WIDE = 128
PLANE = 48
RELAYS = ((45, True), (46, True)) + tuple((p, False) for p in (40, 36, 33, 8, 4, 3))
PIECE = ROWS // len(RELAYS)
EPS = 1e-06


def kernel(
    features,
    sharp_ref,
    bias_ref,
    weights_hbm,
    images_hbm,
    texts_hbm,
    image_grad_ref,
    text_grad_ref,
    row_loss_ref,
    images_ref,
    texts_ref,
    weight_ref,
    near,
    far,
    text,
    grads_near,
    grads_far,
    inverse,
    own_dir,
    near_out,
    near_in,
    far_out,
    far_in,
    back_out,
    back_in,
    carry_out,
    carry_in,
    relay,
    loss_out,
    loss_in,
    far_loss,
    text_sum,
    s_near,
    s_far,
    s_text,
    s_fwd,
    s_ndir,
    s_fdir,
    s_back,
    s_carry,
    s_loss,
    s_relay,
    s_load,
):
    loads = [
        pltpu.make_async_copy(
            images_hbm.at[pl.ds(0, CHUNK)], images_ref.at[pl.ds(0, CHUNK)], s_load.at[0]
        ),
        pltpu.make_async_copy(texts_hbm, texts_ref.at[pl.ds(0, ROWS)], s_load.at[1]),
        pltpu.make_async_copy(
            images_hbm.at[pl.ds(CHUNK, ROWS - CHUNK)],
            images_ref.at[pl.ds(CHUNK, ROWS - CHUNK)],
            s_load.at[2],
        ),
        pltpu.make_async_copy(weights_hbm, weight_ref, s_load.at[3]),
    ]
    for one in loads:
        one.start()
    blk = lax.axis_index("blk")
    member = lax.axis_index("grp")
    groups = lax.axis_size("blk")
    sibling = member + 1 - 2 * lax.rem(member, 2)
    opposite = lax.rem(member + 2, 4)
    diagonal = lax.rem(sibling + 2, 4)
    at_grp = lambda g: {"blk": blk, "grp": g}
    at_blk = lambda b: {"blk": b, "grp": member}
    ahead = lax.rem(blk + 1, groups)
    behind = lax.rem(blk + groups - 1, groups)
    place = lax.rem(blk, PLANE)
    base = blk - place
    next_base = lax.rem(base + PLANE, groups)
    last_base = lax.rem(base + groups - PLANE, groups)
    is_last = place == PLANE - 1
    is_first = place == 0
    is_relay = functools.reduce(jnp.logical_or, [place == p for p, _ in RELAYS])
    piece = sum(j * (place == p).astype(jnp.int32) for j, (p, _) in enumerate(RELAYS))
    at_old = functools.reduce(jnp.logical_or, [place == p for p, old in RELAYS if old])

    def copy(src, dst, sems, k, device):
        return pltpu.make_async_remote_copy(
            src_ref=src,
            dst_ref=dst,
            send_sem=sems.at[0, k],
            recv_sem=sems.at[1, k],
            device_id=device,
            device_id_type=MESH,
        )

    barrier = pltpu.get_barrier_semaphore()

    def greet(device):
        pl.semaphore_signal(barrier, inc=1, device_id=device, device_id_type=MESH)

    for other in (sibling, opposite, diagonal):
        greet(at_grp(other))

    @pl.when(is_first)
    def _():
        for p, old in RELAYS:
            greet(at_blk((last_base if old else base) + p))

    @pl.when(jnp.logical_not(is_first))
    def _():
        greet(at_blk(behind))

    @pl.when(is_relay)
    def _():
        greet(at_blk(jnp.where(at_old, base, last_base) + PLANE - 1))

    near_copy = copy(near.at[pl.ds(0, ROWS)], near.at[pl.ds(ROWS, ROWS)], s_near, 0, at_grp(sibling))

    def far_copy(c):
        return copy(
            near.at[pl.ds(c * CHUNK, CHUNK)],
            far.at[pl.ds(c * WIDE, CHUNK)],
            s_far,
            c,
            at_grp(opposite),
        )

    def forward_copy(c):
        return copy(
            far.at[pl.ds(c * WIDE, CHUNK)],
            far.at[pl.ds(c * WIDE + CHUNK, CHUNK)],
            s_fwd,
            c,
            at_grp(sibling),
        )

    def far_dir_copy(c):
        rows = pl.ds(c * CHUNK, CHUNK)
        return copy(far_out.at[rows], far_in.at[rows], s_fdir, c, at_grp(sibling))

    def back_copy(c):
        rows = pl.ds(c * CHUNK, CHUNK)
        return copy(back_out.at[rows], back_in.at[rows], s_back, c, at_grp(opposite))

    def pass_on(src, dst, start, sems):
        whole = copy(
            src.at[pl.ds(0, ROWS)], dst.at[pl.ds(start, ROWS)], sems, 0, at_blk(ahead)
        )

        @pl.when(is_last)
        def _():
            k = 0 if sems is s_text else 1
            for j, (p, old) in enumerate(RELAYS):
                pltpu.make_async_remote_copy(
                    src_ref=src.at[pl.ds(j * PIECE, PIECE)],
                    dst_ref=relay.at[k],
                    send_sem=sems.at[0, 0],
                    recv_sem=s_relay.at[1, k],
                    device_id=at_blk((base if old else next_base) + p),
                    device_id_type=MESH,
                ).start()

        @pl.when(jnp.logical_not(is_last))
        def _():
            whole.start()

        return whole

    def relay_copy(k, dst, start, sems):
        return pltpu.make_async_remote_copy(
            src_ref=relay.at[k],
            dst_ref=dst.at[pl.ds(pl.multiple_of(start + piece * PIECE, PIECE), PIECE)],
            send_sem=s_relay.at[0, k],
            recv_sem=sems.at[1, 0],
            device_id=at_blk(jnp.where(at_old, next_base, base)),
            device_id_type=MESH,
        )

    def relay_on(k, dst, start, sems):
        @pl.when(is_relay)
        def _():
            copy(relay.at[k], relay.at[k], s_relay, k, at_blk(ahead)).wait_recv()
            relay_copy(k, dst, start, sems).start()

    def unit(values):
        scale = lax.rsqrt(jnp.sum(values * values, axis=-1, keepdims=True) + EPS)
        return values * scale, scale

    def image_rows(c):
        rows = pl.ds(c * CHUNK, CHUNK)
        normed, scale = unit(images_ref[rows, :].astype(jnp.float32))
        near[rows, :] = normed.astype(jnp.bfloat16)
        inverse[rows, :] = jnp.broadcast_to(scale, (CHUNK, 128))

    def text_rows(c):
        rows = pl.ds(c * CHUNK, CHUNK)
        text[rows, :] = unit(texts_ref[rows, :].astype(jnp.float32))[0].astype(jnp.bfloat16)

    loads[0].wait()
    image_rows(0)
    pl.semaphore_wait(barrier, jnp.where(is_last, 3 + len(RELAYS), jnp.where(is_relay, 5, 4)))
    far_copy(0).start()
    text_copy = pass_on(texts_hbm, texts_ref, ROWS, s_text)
    loads[2].wait()
    for c in range(1, CHUNKS):
        image_rows(c)
        far_copy(c).start()

    near_copy.start()
    loads[1].wait()
    for c in range(CHUNKS):
        text_rows(c)
    loads[3].wait()

    sharp = jnp.exp(jnp.full((8, 128), sharp_ref[0], jnp.float32))
    sharp_row = sharp[0:1, :]
    bias = bias_ref[0]

    def pair_terms(products, weights, positive=None):
        logits = sharp_row * products + bias
        decay = jnp.exp(-jnp.abs(logits))
        share = jnp.where(logits >= 0, 1.0, decay) / (1.0 + decay)
        signed = logits
        if positive is not None:
            signed = jnp.where(positive, -logits, logits)
            share = jnp.where(positive, share - 1.0, share)
        losses = jnp.maximum(signed, 0.0) + jnp.log1p(decay)
        return jnp.sum(losses, axis=0, keepdims=True), (weights * share).astype(jnp.bfloat16)

    def against(some_text, some_images):
        return lax.dot_general(
            some_text, some_images, (((1,), (1,)), ((), ())), preferred_element_type=jnp.float32
        )

    def toward(some_grads, some_text):
        return lax.dot_general(
            some_grads, some_text, (((0,), (0,)), ((), ())), preferred_element_type=jnp.float32
        )

    def near_step(k, visit):
        slot, half = k // 2, k % 2
        owner = member if slot == 0 else sibling
        rows = pl.ds(k * WIDE, WIDE)
        texts_at = pl.ds(visit * ROWS, ROWS)
        weights = weight_ref[pl.ds(2 * owner + half, 1), :]
        positive = None
        if visit == 0 and slot == 0:
            shape = (ROWS, WIDE)
            positive = lax.broadcasted_iota(jnp.int32, shape, 0) == (
                lax.broadcasted_iota(jnp.int32, shape, 1) + half * WIDE
            )
        losses, grads = pair_terms(against(text[texts_at, :], near[rows, :]), weights, positive)
        grads_near[texts_at, rows] = grads
        if visit == 0:
            loss_out[slot, pl.ds(half, 1), :] = losses
        else:
            loss_out[slot, pl.ds(half, 1), :] += losses

    def near_dir(k):
        slot, half = k // 2, k % 2
        total = toward(grads_near[:, pl.ds(k * WIDE, WIDE)], text[...])
        rows = pl.ds(half * WIDE, WIDE)
        if slot == 0:
            own_dir[rows, :] = total
        else:
            near_out[rows, :] = total.astype(jnp.bfloat16)

    left = lax.broadcasted_iota(jnp.int32, (1, WIDE), 1) < CHUNK
    swap = lambda row: pltpu.roll(row, CHUNK, 1)

    def far_step(c, visit):
        rows = pl.ds(c * WIDE, WIDE)
        texts_at = pl.ds(visit * ROWS, ROWS)
        one = weight_ref[pl.ds(2 * opposite + c // 2, 1), :]
        two = weight_ref[pl.ds(2 * diagonal + c // 2, 1), :]
        weights = jnp.where(left, one, swap(two)) if c % 2 == 0 else jnp.where(left, swap(one), two)
        losses, grads = pair_terms(against(text[texts_at, :], far[rows, :]), weights)
        grads_far[texts_at, rows] = grads
        if visit == 0:
            far_loss[c, pl.ds(0, 1), :] = losses
        else:
            far_loss[c, pl.ds(0, 1), :] += losses

    def far_dir(c):
        total = toward(grads_far[:, pl.ds(c * WIDE, WIDE)], text[...])
        far_out[pl.ds(c * CHUNK, CHUNK), :] = total[CHUNK:].astype(jnp.bfloat16)
        far_dir_copy(c).start()
        return total[:CHUNK]

    def far_arrives(c):
        far_copy(c).wait_recv()
        forward_copy(c).start()
        forward_copy(c).wait_recv()

    def far_sum(c, mine):
        far_dir_copy(c).wait_recv()
        rows = pl.ds(c * CHUNK, CHUNK)
        back_out[rows, :] = (mine + far_in[rows, :].astype(jnp.float32)).astype(jnp.bfloat16)

    def text_near(visit):
        texts_at = pl.ds(visit * ROWS, ROWS)
        text_sum[texts_at, :] = jnp.dot(
            grads_near[texts_at, :], near[...], preferred_element_type=jnp.float32
        )

    def text_far(visit, rows):
        texts_at = pl.ds(visit * ROWS, ROWS)
        return text_sum[texts_at, :] + jnp.dot(
            grads_far[texts_at, rows], far[rows, :], preferred_element_type=jnp.float32
        )

    early, late = pl.ds(0, 3 * WIDE), pl.ds(3 * WIDE, WIDE)

    near_step(0, 0)
    near_step(1, 0)
    near_copy.wait_recv()
    near_step(2, 0)
    near_step(3, 0)
    relay_on(0, texts_ref, ROWS, s_text)

    near_dir_copy = copy(near_out, near_in, s_ndir, 0, at_grp(sibling))
    for c in range(2):
        far_arrives(c)
        far_step(c, 0)
    text_near(0)

    text_copy.wait_recv()
    for c in range(CHUNKS, 2 * CHUNKS):
        text_rows(c)
    for c in range(CHUNKS):
        if c >= 2:
            far_arrives(c)
            far_step(c, 0)
        if c == CHUNKS - 1:
            carry_out[...] = (sharp[0:1, 0:1] * text_far(0, late)).astype(jnp.bfloat16)
            carry_copy = pass_on(carry_out, carry_in, 0, s_carry)
        far_step(c, 1)
        mine = far_dir(c)
        if c < 2:
            near_step(2 * c, 1)
            near_step(2 * c + 1, 1)
        if c == 2:
            near_dir(2)
            near_dir(3)
            near_dir_copy.start()
            text_sum[pl.ds(0, ROWS), :] = text_far(0, early)
        if c == 3:
            near_dir(0)
            near_dir(1)
        far_sum(c, mine)
        back_copy(c).start()

    for half in range(2):
        even, odd = far_loss[2 * half, 0:1, :], far_loss[2 * half + 1, 0:1, :]
        loss_out[2, pl.ds(half, 1), :] = jnp.where(left, even, swap(odd))
        loss_out[3, pl.ds(half, 1), :] = jnp.where(left, swap(even), odd)
    loss_copies = [
        copy(loss_out.at[k + 1], loss_in.at[k], s_loss, k, at_grp(other))
        for k, other in enumerate((sibling, opposite, diagonal))
    ]
    for one in loss_copies:
        one.start()

    text_near(1)
    text_sum[pl.ds(ROWS, ROWS), :] = sharp[0:1, 0:1] * text_far(1, pl.ds(0, 2 * ROWS))
    relay_on(1, carry_in, 0, s_carry)

    for one in loss_copies:
        one.wait_recv()
    total_loss = loss_out[0] + loss_in[0] + loss_in[1] + loss_in[2]
    row_loss_ref[...] = total_loss[0:2, :] / (STEPS * 4 * ROWS)

    near_dir_copy.wait_recv()
    for c in range(CHUNKS):
        rows = pl.ds(c * CHUNK, CHUNK)
        if c == CHUNKS - 1:
            carry_copy.wait_recv()
            text_grad_ref[...] = (
                text_sum[pl.ds(ROWS, ROWS), :] + carry_in[...].astype(jnp.float32)
            ).astype(jnp.bfloat16)
        back_copy(c).wait_recv()
        step = sharp[0:1, 0:1] * (
            own_dir[rows, :]
            + near_in[rows, :].astype(jnp.float32)
            + back_in[rows, :].astype(jnp.float32)
        )
        scale = inverse[rows, 0:1]
        normed = images_ref[rows, :].astype(jnp.float32) * scale
        image_grad_ref[rows, :] = scale * (
            step - normed * jnp.sum(normed * step, axis=-1, keepdims=True)
        )

    near_copy.wait_send()
    text_copy.wait_send()
    near_dir_copy.wait_send()
    carry_copy.wait_send()
    for one in loss_copies:
        one.wait_send()
    for c in range(CHUNKS):
        far_copy(c).wait_send()
        forward_copy(c).wait_send()
        far_dir_copy(c).wait_send()
        back_copy(c).wait_send()

    @pl.when(is_relay)
    def _():
        relay_copy(0, texts_ref, ROWS, s_text).wait_send()
        relay_copy(1, carry_in, 0, s_carry).wait_send()


def local(images, texts, row_weight, log_sharpness_parameter, bias):
    rows, features = images.shape
    vmem = pl.BlockSpec(memory_space=pltpu.VMEM)
    smem = pl.BlockSpec(memory_space=pltpu.SMEM)
    hbm = pl.BlockSpec(memory_space=pltpu.HBM)
    half = lambda n: pltpu.VMEM((n, features), jnp.bfloat16)
    sems = lambda n: pltpu.SemaphoreType.DMA((2, n))
    stay = [
        pltpu.with_memory_space_constraint(value, pltpu.HBM)
        for value in (row_weight.reshape(8, 128), images, texts)
    ]
    image_grad, text_grad, row_loss = pl.pallas_call(
        functools.partial(kernel, features),
        out_shape=(
            jax.ShapeDtypeStruct((rows, features), jnp.float32),
            jax.ShapeDtypeStruct((rows, features), jnp.bfloat16),
            jax.ShapeDtypeStruct((2, 128), jnp.float32),
        ),
        in_specs=[smem, smem, hbm, hbm, hbm],
        out_specs=(vmem, vmem, vmem),
        scratch_shapes=[
            half(ROWS),
            half(2 * ROWS),
            pltpu.VMEM((8, 128), jnp.float32),
            half(2 * ROWS),
            half(2 * ROWS),
            half(2 * ROWS),
            pltpu.VMEM((2 * ROWS, 2 * ROWS), jnp.bfloat16),
            pltpu.VMEM((2 * ROWS, 2 * ROWS), jnp.bfloat16),
            pltpu.VMEM((ROWS, 128), jnp.float32),
            pltpu.VMEM((ROWS, features), jnp.float32),
            half(ROWS),
            half(ROWS),
            half(ROWS),
            half(ROWS),
            half(ROWS),
            half(ROWS),
            half(ROWS),
            half(ROWS),
            pltpu.VMEM((2, PIECE, features), jnp.bfloat16),
            pltpu.VMEM((4, 8, 128), jnp.float32),
            pltpu.VMEM((3, 8, 128), jnp.float32),
            pltpu.VMEM((CHUNKS, 8, 128), jnp.float32),
            pltpu.VMEM((2 * ROWS, features), jnp.float32),
            sems(1),
            sems(CHUNKS),
            sems(1),
            sems(CHUNKS),
            sems(1),
            sems(CHUNKS),
            sems(CHUNKS),
            sems(1),
            sems(3),
            sems(2),
            pltpu.SemaphoreType.DMA((4,)),
        ],
        compiler_params=pltpu.CompilerParams(
            collective_id=0, has_side_effects=True, vmem_limit_bytes=48 << 20
        ),
        name="pairs",
    )(log_sharpness_parameter, bias, *stay)
    return (image_grad, text_grad, row_loss.reshape(rows))


def solution(mesh):
    placed = (P(("blk", "grp"), None), P(("blk", "grp"), None), P("blk"), P(), P())
    return jax.shard_map(
        local,
        mesh=mesh,
        in_specs=placed,
        out_specs=(P(("blk", "grp"), None), P(("blk", "grp"), None), P(("blk", "grp"))),
        check_vma=False,
    )
```
